32 devices in a mesh: dp: 4 (over y, x), expert: 4 (over z), tensor: 2 (over core).
Axes of the slice: x: 2, y: 2, z: 4, core: 2. Of those that a mesh axis runs over, the one named last changes fastest.
Arguments:
- tokens: bfloat16 [2048, 4096], P('expert', 'dp'), may hold values from -6 to 6
- labels: int32 [2048, 1], P('expert'), may hold values from 0 to 7; in each aligned block of 512 rows (0 to 511, 512 to 1023, ...) at most 96 rows name the same one
- grad_out: bfloat16 [2048, 4096], P('expert', 'dp'), may hold values from -1.5 to 1.5
- w_gate: bfloat16 [8, 4096, 7168], P('expert', 'dp', 'tensor'), may hold values from -0.09375 to 0.09375
- w_up: bfloat16 [8, 4096, 7168], P('expert', 'dp', 'tensor'), may hold values from -0.09375 to 0.09375
- w_down: bfloat16 [8, 7168, 4096], P('expert', 'tensor', 'dp'), may hold values from -0.0625 to 0.0625
Outputs:
- mixed: bfloat16 [2048, 4096], P('expert', 'dp')
- grad_tokens: bfloat16 [2048, 4096], P('expert', 'dp')
- grad_gate: bfloat16 [8, 4096, 7168], P('expert', 'dp', 'tensor')
- grad_up: bfloat16 [8, 4096, 7168], P('expert', 'dp', 'tensor')
- grad_down: bfloat16 [8, 7168, 4096], P('expert', 'tensor', 'dp')
The draws below stay inside these ranges and needn't reach their ends.
Inputs may be any that keep to these rules, and one draw needn't show every extreme that they name: `labels`: in each aligned block of 512 rows (the rows of one index of expert) no domain appears more than 96 times; some domain appears exactly 96 times in some block. Every domain appears somewhere.
All inputs are finite; a program needn't handle non-finite values.
Results may differ from the reference program's by a relative error of at most 0.005.
Values may be sent and summed in bfloat16 or wider, within the bound.
No kernel may reach another device: no remote copies, remote signals or barrier semaphores. Data moves between devices by JAX's collectives and lax.ppermute only.
A program may use at most 192 MiB of HBM per device.

```python
import math
import jax
import jax.numpy as jnp
import numpy as np
from jax import lax

D = 4096
FF = 7168
TOK_DEV = 512
MOST = 96
EXPERTS = 8
TOKENS = 2048


def levels(stream_key, extent, split, low, high):
    def one(dim, blocks):
        heights = jax.random.uniform(jax.random.fold_in(jax.random.fold_in(stream_key, 6), dim), (blocks,), jnp.float32, low / len(split), high / len(split))
        return jnp.repeat(jnp.exp(heights), extent[dim] // blocks).reshape((-1,) + (1,) * (len(extent) - dim - 1))

    loudness = one(*split[0])
    for cut in split[1:]:
        loudness = loudness * one(*cut)
    return loudness


def deal_out(key, own, number, rows, amount, top, most, lean):
    ranking = jax.random.permutation(key, amount)
    heavy_load, common = portions_of(amount, rows * top, most, lean, True), portions_of(amount, rows * top, most, lean, False)
    places = jnp.arange(amount)

    def named(sizes, rotation):
        used = int((sizes > 0).sum())
        fixed = max(1, used // 4)
        moved = fixed + (places - fixed + rotation * (used - fixed)) % max(1, amount - fixed)
        return jnp.zeros((amount,), jnp.int32).at[ranking[jnp.where(places < fixed, places, moved)]].set(jnp.asarray(sizes, jnp.int32))

    sizes = jnp.where(number % 4 == 0, named(heavy_load, number // 4), named(common, number - number // 4 - 1))
    mixed = jax.random.permutation(jax.random.fold_in(own, 3), amount)
    giver, receiver = mixed[0:amount // 2 * 2:2], mixed[1:amount // 2 * 2:2]
    slack = jnp.minimum(sizes[giver] - 1, most - sizes[receiver]) // 2
    slack = jnp.where((giver == ranking[0]) | (receiver == ranking[0]) | (sizes[receiver] == 0), 0, jnp.maximum(slack, 0))
    moved = jax.random.randint(jax.random.fold_in(own, 4), (amount // 2,), 0, 1 << 20) % (slack + 1)
    sizes = sizes.at[giver].add(-moved).at[receiver].add(moved)
    items = jnp.searchsorted(jnp.cumsum(sizes), jnp.arange(rows * top), side="right").astype(jnp.int32)
    grid = items.reshape(top, rows).T
    grid = grid[jax.random.permutation(jax.random.fold_in(own, 1), rows)]
    rotation = jax.random.randint(jax.random.fold_in(own, 2), (rows, 1), 0, top)
    return jnp.take_along_axis(grid, (jnp.arange(top)[None, :] + rotation) % top, axis=1)


def portions_of(count, total, reach, lean, full):
    loads = [(1 << 20) // math.isqrt(rank ** lean) + 1 for rank in range(1, count + 1)]
    largest = reach if full else min(reach, max(-(-total // count), total * loads[0] // sum(loads)))
    least = 1 if total - largest >= count - 1 else 0
    counts, spare = [largest] + [least] * (count - 1), total - largest - least * (count - 1)
    while spare > 0:
        movable = [i for i in range(1, count) if counts[i] < largest] or [i for i in range(1, count) if counts[i] < reach]
        pool, budget = sum([loads[i] for i in movable]), spare
        for i in movable:
            addition = min(reach - counts[i], max(1, budget * loads[i] // pool), spare)
            counts[i] = counts[i] + addition
            spare = spare - addition
    return np.array(counts)


def scatter_about(stream_key, shape, width, limit, cuts=(), kind=jnp.bfloat16):
    level = levels(stream_key, shape, cuts, -0.22, 0.18) if cuts else 1.0
    result = jax.random.normal(stream_key, shape, jnp.float32) * width * level
    return jnp.minimum(jnp.maximum(result, -limit), limit).astype(kind)


def setup_inputs(seed: int = 0) -> dict:
    arg_keys = jax.random.split(jax.random.key(seed), 7)
    tokens = scatter_about(arg_keys[0], (TOKENS, D), 1.0, 6.0, ((0, 4), (1, 4)))
    labels_keys = jax.random.split(jax.random.fold_in(arg_keys[1], 1), TOKENS // TOK_DEV)
    labels_turns = jax.random.permutation(jax.random.fold_in(arg_keys[1], 3), TOKENS // TOK_DEV)
    labels = jax.vmap(lambda own, number: deal_out(jax.random.fold_in(arg_keys[1], 2), own, number, TOK_DEV, EXPERTS, 1, MOST, 2))(labels_keys, labels_turns).reshape((TOKENS, 1))
    grad_out = scatter_about(arg_keys[2], (TOKENS, D), 0.25, 1.5, ((0, 4), (1, 4)))
    w_gate = scatter_about(arg_keys[3], (EXPERTS, D, FF), D ** -0.5, 0.09375, ((0, 4), (1, 4), (2, 2)))
    w_up = scatter_about(arg_keys[4], (EXPERTS, D, FF), D ** -0.5, 0.09375, ((0, 4), (1, 4), (2, 2)))
    w_down = scatter_about(arg_keys[5], (EXPERTS, FF, D), FF ** -0.5, 0.0625, ((0, 4), (1, 2), (2, 4)))
    return dict(tokens=tokens, labels=labels, grad_out=grad_out, w_gate=w_gate, w_up=w_up, w_down=w_down)


def reference(tokens, labels, grad_out, w_gate, w_up, w_down):
    domain = labels[:, 0]
    capacity = MOST * (TOKENS // TOK_DEV)

    def per_expert(expert):
        hits = domain == expert
        row_index = jnp.nonzero(hits, size=capacity, fill_value=0)[0].astype(jnp.int32)
        tally = jnp.sum(hits.astype(jnp.int32))
        is_valid = (jnp.arange(capacity, dtype=jnp.int32) < tally).astype(jnp.bfloat16)
        expert_in = tokens[row_index] * is_valid[:, None]
        expert_grad = grad_out[row_index] * is_valid[:, None]
        gate_w = w_gate[expert]
        up_w = w_up[expert]
        down_w = w_down[expert]
        gate_sum = jnp.dot(expert_in, gate_w, preferred_element_type=jnp.float32)
        up_sum = jnp.dot(expert_in, up_w, preferred_element_type=jnp.float32)
        back_sum = jnp.dot(expert_grad, down_w.T, preferred_element_type=jnp.float32)
        sigmoid_gate = jax.nn.sigmoid(gate_sum)
        active = gate_sum * sigmoid_gate
        hidden = (active * up_sum).astype(jnp.bfloat16)
        d_gate = (back_sum * up_sum * (sigmoid_gate * (1.0 + gate_sum * (1.0 - sigmoid_gate)))).astype(jnp.bfloat16)
        d_up = (back_sum * active).astype(jnp.bfloat16)
        out_rows = jnp.dot(hidden, down_w, preferred_element_type=jnp.float32)
        in_grad = jnp.dot(d_gate, gate_w.T, preferred_element_type=jnp.float32) + jnp.dot(d_up, up_w.T, preferred_element_type=jnp.float32)
        grad_g = jnp.dot(expert_in.T, d_gate, preferred_element_type=jnp.float32).astype(jnp.bfloat16)
        grad_u = jnp.dot(expert_in.T, d_up, preferred_element_type=jnp.float32).astype(jnp.bfloat16)
        grad_d = jnp.dot(hidden.T, expert_grad, preferred_element_type=jnp.float32).astype(jnp.bfloat16)
        keep = is_valid.astype(jnp.float32)[:, None]
        return row_index, out_rows * keep, in_grad * keep, grad_g, grad_u, grad_d

    row_index, out_rows, in_grad, grad_gate, grad_up, grad_down = lax.map(per_expert, jnp.arange(EXPERTS, dtype=jnp.int32))
    flat_index = row_index.reshape(-1)
    mixed = jnp.zeros((TOKENS, D), jnp.float32).at[flat_index].add(out_rows.reshape(-1, D))
    grad_tokens = jnp.zeros((TOKENS, D), jnp.float32).at[flat_index].add(in_grad.reshape(-1, D))
    return mixed.astype(jnp.bfloat16), grad_tokens.astype(jnp.bfloat16), grad_gate, grad_up, grad_down
```

```python
import jax
import jax.numpy as jnp
from jax import lax
from jax.sharding import PartitionSpec as P

MOST = 96
BF16 = jnp.bfloat16
F32 = jnp.float32


def dot(lhs, rhs, lhs_dim, rhs_dim):
    return lax.dot_general(lhs, rhs, (((lhs_dim,), (rhs_dim,)), ((), ())), preferred_element_type=F32)


def after(value, *others):
    return lax.optimization_barrier((value, others))[0]


def body(tokens, labels, grad_out, w_gate, w_up, w_down):
    local = w_gate.shape[0]
    groups = lax.axis_size("expert")
    cores = lax.axis_size("tensor")
    peers = lax.axis_size("dp")
    experts = local * groups
    rows = groups * MOST
    half, quarter = rows // 2, rows // 4
    share = MOST // cores
    part = MOST // 4
    paired = cores == 2
    me = lax.axis_index("dp")
    group = lax.axis_index("expert")
    core = lax.axis_index("tensor")

    def over_dp(value, bit):
        return lax.ppermute(value, "dp", [(i, i ^ bit) for i in range(peers)])

    def over_groups(value, shift):
        return lax.ppermute(value, "expert", [(i, (i + shift) % groups) for i in range(groups)])

    def other_core(value):
        return lax.ppermute(value, "tensor", [(0, 1), (1, 0)])

    first = [1 + j % 2 for j in range(local)]
    second = [2 - j % 2 for j in range(local)]

    domain = labels[:, 0]
    onehot = domain[:, None] == jnp.arange(experts, dtype=jnp.int32)[None, :]
    count = domain.shape[0]
    ahead = (jnp.arange(count)[:, None] > jnp.arange(count)[None, :]).astype(BF16)
    before = dot(ahead, onehot.astype(BF16), 1, 0)
    rank_in = jnp.sum(jnp.where(onehot, before, 0.0), axis=1).astype(jnp.int32)
    slot_of = rank_in * experts + domain

    def slots_held(of_core):
        place = jnp.arange(share, dtype=jnp.int32)[None, None, :]
        if not paired:
            place = place + of_core * share
        expert_in = jnp.arange(local, dtype=jnp.int32)[None, :, None]
        to_group = (group + jnp.arange(groups, dtype=jnp.int32)[:, None, None]) % groups
        bit_first = 1 + expert_in % 2
        bit_second = 2 - expert_in % 2
        position = place // part
        owner = (position // 2) * bit_first + (position % 2) * bit_second
        owner = owner ^ me
        if paired:
            owner = owner ^ (of_core * bit_first)
        rank = owner * part + place % part
        return (rank * experts + to_group * local + expert_in).reshape(-1)

    own_slots = slots_held(core)
    to_slots = (own_slots[:, None] == slot_of[None, :]).astype(BF16)

    def send_out(value):
        packed = dot(to_slots, value, 1, 0).astype(BF16).reshape(groups, local, share, -1)
        return [packed[0]] + [over_groups(packed[k], k) for k in range(1, groups)]

    def take_in(arrived):
        mine = jnp.stack(arrived)
        if paired:
            both = jnp.stack([mine, other_core(mine)])
        else:
            both = lax.all_gather(mine, "tensor", axis=0, tiled=False)
        inner = min(share, part)
        both = both.reshape(cores, groups, local, share // inner, inner, -1)
        both = both.transpose(2, 0, 3, 1, 4, 5).reshape(local, rows, -1)
        return [both[j] for j in range(local)]

    def send_half(source, weight, dim):
        return [dot(source[j][half:], weight[j], 1, dim).astype(BF16) for j in range(local)]

    def keep_half(source, weight, dim):
        return [dot(source[j][:half], weight[j], 1, dim) for j in range(local)]

    def step_one(sent):
        return [over_dp(sent[j], first[j]) for j in range(local)]

    def step_two(kept, got):
        sums = []
        for j in range(local):
            passed = (kept[j][quarter:] + got[j][quarter:].astype(F32)).astype(BF16)
            last = over_dp(passed, second[j])
            sums.append(kept[j][:quarter] + got[j][:quarter].astype(F32) + last.astype(F32))
        return sums

    def gather_rows(owned):
        full = []
        for j in range(local):
            a = owned[j]
            b = over_dp(a, second[j])
            c = over_dp(a, first[j])
            d = over_dp(b, first[j])
            full.append((a, b, c, d))
        return full

    def joined(pieces):
        return [jnp.concatenate(p, axis=0) for p in pieces]

    def share_rows(value):
        stacked = jnp.stack(value)
        width = stacked.shape[-1]
        if paired:
            summed = stacked[:, :half] + other_core(stacked[:, half:])
        else:
            summed = lax.psum_scatter(stacked, "tensor", scatter_dimension=1, tiled=True)
        inner = min(share, part)
        summed = summed.astype(BF16).reshape(local, share // inner, groups, inner, width)
        blocks = summed.transpose(2, 0, 1, 3, 4).reshape(groups, local, share, width)
        home = [blocks[0]] + [over_groups(blocks[k], -k) for k in range(1, groups)]
        return jnp.stack(home).reshape(groups * local * share, width)

    def to_tokens(home):
        if paired:
            every = jnp.concatenate([home, other_core(home)], axis=0)
            held = jnp.concatenate([own_slots, slots_held(1 - core)])
        else:
            every = lax.all_gather(home, "tensor", axis=0, tiled=True)
            held = jnp.concatenate([slots_held(c) for c in range(cores)])
        from_slots = (slot_of[:, None] == held[None, :]).astype(BF16)
        return dot(from_slots, every, 1, 0).astype(BF16)

    inputs = take_in(send_out(tokens))
    gate_sent = send_half(inputs, w_gate, 0)
    gate_got = step_one(gate_sent)
    grads_out = send_out(after(grad_out, inputs))
    up_sent = send_half(inputs, w_up, 0)
    up_got = step_one(up_sent)
    gate_kept = keep_half(after(inputs, up_sent), w_gate, 0)
    grad_rows = take_in(after(grads_out, gate_kept))
    up_kept = keep_half(inputs, w_up, 0)
    back_sent = send_half(grad_rows, w_down, 1)
    back_got = step_one(after(back_sent, gate_got))
    gate_sum = step_two(gate_kept, gate_got)
    back_kept = keep_half(grad_rows, w_down, 1)
    up_sum = step_two(up_kept, up_got)

    hidden = []
    for j in range(local):
        hidden.append((gate_sum[j] * jax.nn.sigmoid(gate_sum[j]) * up_sum[j]).astype(BF16))
    hidden_pieces = gather_rows(hidden)
    back_sum = step_two(back_kept, back_got)
    d_gate, d_up = [], []
    for j in range(local):
        g, u, b = gate_sum[j], up_sum[j], back_sum[j]
        s = jax.nn.sigmoid(g)
        d_gate.append((b * u * (s * (1.0 + g * (1.0 - s)))).astype(BF16))
        d_up.append((b * (g * s)).astype(BF16))

    gate_pieces = gather_rows(after(d_gate, [p[2] for p in hidden_pieces]))
    hidden_rows = joined(hidden_pieces)
    forward = [dot(hidden_rows[j], w_down[j], 1, 0) for j in range(local)]
    mixed = to_tokens(share_rows(forward))
    up_pieces = gather_rows(after(d_up, [p[2] for p in gate_pieces]))
    gate_rows = joined(gate_pieces)
    up_rows = joined(up_pieces)
    backward = [dot(gate_rows[j], w_gate[j], 1, 1) + dot(up_rows[j], w_up[j], 1, 1) for j in range(local)]

    def outer(left, right):
        return jnp.einsum(
            "jrd,jrf->jdf", jnp.stack(left), jnp.stack(right), preferred_element_type=F32
        ).astype(BF16)

    grad_down = outer(hidden_rows, grad_rows)
    grad_gate = outer(inputs, after(gate_rows, mixed))
    grad_home = share_rows(backward)
    grad_up = outer(inputs, after(up_rows, backward))
    grad_tokens = to_tokens(grad_home)
    return mixed, grad_tokens, grad_gate, grad_up, grad_down


def solution(mesh):
    in_specs = (
        P("expert", "dp"),
        P("expert", None),
        P("expert", "dp"),
        P("expert", "dp", "tensor"),
        P("expert", "dp", "tensor"),
        P("expert", "tensor", "dp"),
    )
    out_specs = (
        P("expert", "dp"),
        P("expert", "dp"),
        P("expert", "dp", "tensor"),
        P("expert", "dp", "tensor"),
        P("expert", "tensor", "dp"),
    )
    return jax.shard_map(body, mesh=mesh, in_specs=in_specs, out_specs=out_specs, check_vma=False)
```

```python
import jax
import jax.numpy as jnp
from jax import lax
from jax.experimental import pallas as pl
from jax.experimental.pallas import tpu as pltpu
from jax.sharding import PartitionSpec as P

MOST = 96
BF16 = jnp.bfloat16
F32 = jnp.float32


def dot(lhs, rhs, lhs_dim, rhs_dim):
    return lax.dot_general(lhs, rhs, (((lhs_dim,), (rhs_dim,)), ((), ())), preferred_element_type=F32)


VMEM = 56 * 1024 * 1024


def kernel_params(flops, moved):
    return dict(
        compiler_params=pltpu.CompilerParams(vmem_limit_bytes=VMEM),
        cost_estimate=pl.CostEstimate(flops=flops, bytes_accessed=moved, transcendentals=0),
    )


def unread(values):
    return [pl.BlockSpec(memory_space=pl.ANY)] * len(values)


def tile_of(width):
    return width // 2 if width % 256 == 0 else width


def back_to_rows(pieces, weight, j, dim, added=(), waits=()):
    width = pieces[0].shape[1]
    sizes = [p.shape[0] for p in pieces]
    rows = sum(sizes)
    half = rows // 2
    feat = weight.shape[2 - dim]
    tile = tile_of(width)
    count = len(pieces)

    def kernel(*refs):
        parts, w_ref, start = refs[:count], refs[count], refs[count + 1 : count + 1 + len(added)]
        low_ref, high_ref = refs[-2:]

        @pl.when(pl.program_id(0) == 0)
        def _():
            low_ref[...] = start[0][...] if start else jnp.zeros_like(low_ref)
            high_ref[...] = start[1][...] if start else jnp.zeros_like(high_ref)

        x = jnp.concatenate([p[...] for p in parts], axis=0)
        total = dot(x, w_ref[0], 1, dim)
        low_ref[...] += total[:half]
        high_ref[...] += total[half:]

    if dim == 0:
        weight_spec = pl.BlockSpec((1, tile, feat), lambda i: (j, i, 0))
    else:
        weight_spec = pl.BlockSpec((1, feat, tile), lambda i: (j, 0, i))
    whole = pl.BlockSpec((half, feat), lambda i: (0, 0))
    return pl.pallas_call(
        kernel,
        grid=(width // tile,),
        in_specs=[pl.BlockSpec((n, tile), lambda i: (0, i)) for n in sizes] + [weight_spec] + [whole] * len(added) + unread(waits),
        out_specs=[whole] * 2,
        out_shape=[jax.ShapeDtypeStruct((half, feat), F32)] * 2,
        name="back_to_rows",
        **kernel_params(2 * rows * feat * width, 2 * feat * width + 2 * rows * width + 4 * rows * feat),
    )(*pieces, weight, *added, *waits)


def outer(x, pieces, shape, j, into, x_first, waits=(), brief=False):
    width = pieces[0].shape[1]
    sizes = [p.shape[0] for p in pieces]
    rows = sum(sizes)
    feat = x.shape[0] if x_first else x.shape[1]
    tile = tile_of(width)
    count = len(pieces)

    def kernel(*refs):
        x_ref, parts, out_ref = refs[0], refs[1 : 1 + count], refs[-1]
        y = jnp.concatenate([p[...] for p in parts], axis=0)
        if x_first:
            out_ref[0] = dot(x_ref[...], y, 1, 0).astype(BF16)
        else:
            out_ref[0] = dot(y, x_ref[...], 0, 0).astype(BF16)

    if x_first:
        out_spec = pl.BlockSpec((1, feat, tile), lambda i: (j, 0, i))
    else:
        out_spec = pl.BlockSpec((1, tile, feat), lambda i: (j, i, 0))
    return pl.pallas_call(
        kernel,
        grid=(width // tile,),
        in_specs=[pl.BlockSpec(x.shape, lambda i: (0, 0))]
        + [pl.BlockSpec((n, tile), lambda i: (0, i)) for n in sizes]
        + unread(into)
        + unread(waits),
        out_specs=out_spec,
        out_shape=jax.ShapeDtypeStruct(shape, BF16),
        input_output_aliases={1 + count: 0} if into else {},
        name="outer",
        **(kernel_params(0, 0) if brief else kernel_params(2 * rows * feat * width, 2 * feat * width + 2 * rows * width)),
    )(x, *pieces, *into, *waits)


def spaced(*values):
    def kernel(*refs):
        refs[-1][...] = jnp.zeros_like(refs[-1])

    return pl.pallas_call(
        kernel,
        in_specs=unread(values),
        out_specs=pl.BlockSpec(memory_space=pltpu.VMEM),
        out_shape=jax.ShapeDtypeStruct((8, 128), F32),
        name="spaced",
        cost_estimate=pl.CostEstimate(flops=0, bytes_accessed=1 << 27, transcendentals=0),
    )(*values)


def gathered(values, waits):
    count = len(values)
    shape = (count,) + values[0].shape

    def kernel(*refs):
        for n in range(count):
            refs[-1][n] = refs[n][...]

    return pl.pallas_call(
        kernel,
        in_specs=[pl.BlockSpec(memory_space=pltpu.VMEM)] * count + unread(waits),
        out_specs=pl.BlockSpec(memory_space=pltpu.VMEM),
        out_shape=jax.ShapeDtypeStruct(shape, values[0].dtype),
        name="gathered",
        **kernel_params(0, 4 * count * values[0].size),
    )(*values, *waits)


def held(value, *waits):
    def kernel(*refs):
        refs[-1][...] = refs[0][...]

    return pl.pallas_call(
        kernel,
        in_specs=[pl.BlockSpec(memory_space=pltpu.VMEM)] + unread(waits),
        out_specs=pl.BlockSpec(memory_space=pltpu.VMEM),
        out_shape=jax.ShapeDtypeStruct(value.shape, value.dtype),
        name="held",
        **kernel_params(0, 4 * value.size),
    )(value, *waits)


def body(tokens, labels, grad_out, w_gate, w_up, w_down):
    local = w_gate.shape[0]
    groups = lax.axis_size("expert")
    cores = lax.axis_size("tensor")
    peers = lax.axis_size("dp")
    experts = local * groups
    rows = groups * MOST
    half, quarter = rows // 2, rows // 4
    share = MOST // cores
    part = MOST // 4
    paired = cores == 2
    me = lax.axis_index("dp")
    group = lax.axis_index("expert")
    core = lax.axis_index("tensor")

    def over_dp(value, bit):
        return lax.ppermute(value, "dp", [(i, i ^ bit) for i in range(peers)])

    def over_groups(value, shift):
        return lax.ppermute(value, "expert", [(i, (i + shift) % groups) for i in range(groups)])

    def other_core(value):
        return lax.ppermute(value, "tensor", [(0, 1), (1, 0)])

    first = [1 + j % 2 for j in range(local)]
    second = [2 - j % 2 for j in range(local)]

    domain = labels[:, 0]
    onehot = domain[:, None] == jnp.arange(experts, dtype=jnp.int32)[None, :]
    count = domain.shape[0]
    ahead = (jnp.arange(count)[:, None] > jnp.arange(count)[None, :]).astype(BF16)
    before = dot(ahead, onehot.astype(BF16), 1, 0)
    rank_in = jnp.sum(jnp.where(onehot, before, 0.0), axis=1).astype(jnp.int32)
    slot_of = rank_in * experts + domain

    def slots_held(of_core):
        place = jnp.arange(share, dtype=jnp.int32)[None, None, :]
        if not paired:
            place = place + of_core * share
        expert_in = jnp.arange(local, dtype=jnp.int32)[None, :, None]
        to_group = (group + jnp.arange(groups, dtype=jnp.int32)[:, None, None]) % groups
        bit_first = 1 + expert_in % 2
        bit_second = 2 - expert_in % 2
        position = place // part
        owner = (position // 2) * bit_first + (position % 2) * bit_second
        owner = owner ^ me
        if paired:
            owner = owner ^ (of_core * bit_first)
        rank = owner * part + place % part
        return (rank * experts + to_group * local + expert_in).reshape(-1)

    own_slots = slots_held(core)
    to_slots = (own_slots[:, None] == slot_of[None, :]).astype(BF16)

    def send_out(value):
        packed = dot(to_slots, value, 1, 0).astype(BF16).reshape(groups, local, share, -1)
        return [packed[0]] + [over_groups(packed[k], k) for k in range(1, groups)]

    def take_in(arrived):
        mine = jnp.stack(arrived)
        if paired:
            both = jnp.stack([mine, other_core(mine)])
        else:
            both = lax.all_gather(mine, "tensor", axis=0, tiled=False)
        inner = min(share, part)
        both = both.reshape(cores, groups, local, share // inner, inner, -1)
        both = both.transpose(2, 0, 3, 1, 4, 5).reshape(local, rows, -1)
        return [both[j] for j in range(local)]

    def send_half(source, weight, dim):
        return [dot(source[j][half:], weight[j], 1, dim).astype(BF16) for j in range(local)]

    def keep_half(source, weight, dim):
        return [dot(source[j][:half], weight[j], 1, dim) for j in range(local)]

    def step_one(sent):
        return [over_dp(sent[j], first[j]) for j in range(local)]

    def passed_on(kept, got):
        return [(kept[j][quarter:] + got[j][quarter:].astype(F32)).astype(BF16) for j in range(local)]

    def step_two(kept, got, passed):
        last = [over_dp(passed[j], second[j]) for j in range(local)]
        return [
            kept[j][:quarter] + got[j][:quarter].astype(F32) + last[j].astype(F32) for j in range(local)
        ]

    def along_second(value):
        return [over_dp(value[j], second[j]) for j in range(local)]

    def along_first(value):
        return [over_dp(value[j], first[j]) for j in range(local)]

    def rows_of(pieces, weight, dim, added=None, waits=()):
        return [
            back_to_rows(pieces[j], weight, j, dim, added[j] if added else (), waits) for j in range(local)
        ]

    def outer_all(source, pieces, shape, x_first, waits=(), brief=False):
        total = ()
        for j in range(local):
            total = (outer(source[j], pieces[j], shape, j, total, x_first, waits, brief),)
        return total[0]

    def share_blocks(value):
        width = value[0][0].shape[-1]
        if paired:
            summed = jnp.stack([low + other_core(high) for low, high in value])
        else:
            stacked = jnp.stack([jnp.concatenate(v, axis=0) for v in value])
            summed = lax.psum_scatter(stacked, "tensor", scatter_dimension=1, tiled=True)
        inner = min(share, part)
        summed = summed.astype(BF16).reshape(local, share // inner, groups, inner, width)
        blocks = summed.transpose(2, 0, 1, 3, 4).reshape(groups, local, share, width)
        return [blocks[k] for k in range(groups)]

    def return_home(blocks):
        return [blocks[0]] + [over_groups(blocks[k], -k) for k in range(1, groups)]

    def to_tokens(home):
        if paired:
            every = jnp.concatenate([home, other_core(home)], axis=0)
            held = jnp.concatenate([own_slots, slots_held(1 - core)])
        else:
            every = lax.all_gather(home, "tensor", axis=0, tiled=True)
            held = jnp.concatenate([slots_held(c) for c in range(cores)])
        from_slots = (slot_of[:, None] == held[None, :]).astype(BF16)
        return dot(from_slots, every, 1, 0).astype(BF16)

    inputs = take_in(send_out(tokens))
    gate_sent = send_half(inputs, w_gate, 0)
    gate_sent = list(lax.optimization_barrier(tuple(gate_sent)))
    gate_got = step_one(gate_sent)
    up_sent = send_half(inputs, w_up, 0)
    up_sent = list(lax.optimization_barrier(tuple(up_sent)))
    up_got = step_one(up_sent)
    grads_out = send_out(held(grad_out, *gate_sent))
    gate_kept = keep_half(inputs, w_gate, 0)
    gate_passed = passed_on(gate_kept, gate_got)
    gate_sum = step_two(gate_kept, gate_got, gate_passed)
    grad_rows = take_in(grads_out)
    up_kept = keep_half(inputs, w_up, 0)
    back_sent = send_half(grad_rows, w_down, 1)
    back_sent = list(lax.optimization_barrier(tuple(back_sent)))
    back_got = step_one(back_sent)
    back_kept = keep_half(grad_rows, w_down, 1)
    up_passed = passed_on(up_kept, up_got)
    up_sum = step_two(up_kept, up_got, up_passed)
    back_passed = passed_on(back_kept, back_got)

    hidden = []
    for j in range(local):
        hidden.append((gate_sum[j] * jax.nn.sigmoid(gate_sum[j]) * up_sum[j]).astype(BF16))
    h_second, h_first = along_second(hidden), along_first(hidden)
    back_sum = step_two(back_kept, back_got, back_passed)
    d_gate, d_up = [], []
    for j in range(local):
        g, u, b = gate_sum[j], up_sum[j], back_sum[j]
        s = jax.nn.sigmoid(g)
        d_gate.append((b * u * (s * (1.0 + g * (1.0 - s)))).astype(BF16))
        d_up.append((b * (g * s)).astype(BF16))

    h_both = along_first(h_second)
    late = [held(v, *h_both) for v in d_gate]
    g_second, g_first = along_second(late), along_first(late)
    hidden_pieces = list(zip(hidden, h_second, h_first, h_both))
    forward = rows_of(hidden_pieces, w_down, 0, None, g_second)
    g_both = along_first(g_second)
    late = d_up
    u_second, u_first = along_second(late), along_first(late)
    grad_down = outer_all(grad_rows, hidden_pieces, w_down.shape, False, [f[0] for f in forward] + u_second)
    gate_pieces = list(zip(d_gate, g_second, g_first, g_both))
    by_gate = rows_of(gate_pieces, w_gate, 1, None, ())
    inputs_t = [x.T for x in inputs]
    grad_gate = outer_all(inputs_t, gate_pieces, w_gate.shape, True, [grad_down])
    u_both = along_first([held(v, *[grad_down]) for v in u_second])
    mixed_home = jnp.stack(return_home(share_blocks([(held(low, *g_both), high) for low, high in forward]))).reshape(
        groups * local * share, -1
    )
    mixed = to_tokens(mixed_home)
    up_pieces = list(zip(d_up, u_second, u_first, u_both))
    backward = rows_of(up_pieces, w_up, 1, by_gate, [grad_gate] + [mixed])
    grad_blocks = share_blocks(backward)
    grad_up = outer_all(inputs_t, up_pieces, w_up.shape, True, [spaced(*grad_blocks)], True)
    grad_home = gathered(return_home(grad_blocks), [grad_up])
    grad_tokens = to_tokens(grad_home.reshape(groups * local * share, -1))
    return mixed, grad_tokens, grad_gate, grad_up, grad_down


def solution(mesh):
    in_specs = (
        P("expert", "dp"),
        P("expert", None),
        P("expert", "dp"),
        P("expert", "dp", "tensor"),
        P("expert", "dp", "tensor"),
        P("expert", "tensor", "dp"),
    )
    out_specs = (
        P("expert", "dp"),
        P("expert", "dp"),
        P("expert", "dp", "tensor"),
        P("expert", "dp", "tensor"),
        P("expert", "tensor", "dp"),
    )
    return jax.shard_map(body, mesh=mesh, in_specs=in_specs, out_specs=out_specs, check_vma=False)
```

```python
import jax
import jax.numpy as jnp
from jax import lax
from jax.experimental import pallas as pl
from jax.experimental.pallas import tpu as pltpu
from jax.sharding import PartitionSpec as P

MOST = 96
BF16 = jnp.bfloat16
F32 = jnp.float32


def dot(lhs, rhs, lhs_dim, rhs_dim):
    return lax.dot_general(lhs, rhs, (((lhs_dim,), (rhs_dim,)), ((), ())), preferred_element_type=F32)


VMEM = 56 * 1024 * 1024


def kernel_params(flops, moved):
    return dict(
        compiler_params=pltpu.CompilerParams(vmem_limit_bytes=VMEM),
        cost_estimate=pl.CostEstimate(flops=flops, bytes_accessed=moved, transcendentals=0),
    )


def unread(values):
    return [pl.BlockSpec(memory_space=pl.ANY)] * len(values)


def tile_of(width):
    return width // 2 if width % 256 == 0 else width


def back_to_rows(pieces, weight, j, dim, added=(), waits=()):
    width = pieces[0].shape[1]
    sizes = [p.shape[0] for p in pieces]
    rows = sum(sizes)
    half = rows // 2
    feat = weight.shape[2 - dim]
    tile = tile_of(width)
    count = len(pieces)

    def kernel(*refs):
        parts, w_ref, start = refs[:count], refs[count], refs[count + 1 : count + 1 + len(added)]
        low_ref, high_ref = refs[-2:]

        @pl.when(pl.program_id(0) == 0)
        def _():
            low_ref[...] = start[0][...] if start else jnp.zeros_like(low_ref)
            high_ref[...] = start[1][...] if start else jnp.zeros_like(high_ref)

        x = jnp.concatenate([p[...] for p in parts], axis=0)
        total = dot(x, w_ref[0], 1, dim)
        low_ref[...] += total[:half]
        high_ref[...] += total[half:]

    if dim == 0:
        weight_spec = pl.BlockSpec((1, tile, feat), lambda i: (j, i, 0))
    else:
        weight_spec = pl.BlockSpec((1, feat, tile), lambda i: (j, 0, i))
    whole = pl.BlockSpec((half, feat), lambda i: (0, 0))
    return pl.pallas_call(
        kernel,
        grid=(width // tile,),
        in_specs=[pl.BlockSpec((n, tile), lambda i: (0, i)) for n in sizes] + [weight_spec] + [whole] * len(added) + unread(waits),
        out_specs=[whole] * 2,
        out_shape=[jax.ShapeDtypeStruct((half, feat), F32)] * 2,
        name="back_to_rows",
        **kernel_params(2 * rows * feat * width, 2 * feat * width + 2 * rows * width + 4 * rows * feat),
    )(*pieces, weight, *added, *waits)


def outer(x, pieces, shape, j, into, x_first, waits=(), brief=False):
    width = pieces[0].shape[1]
    sizes = [p.shape[0] for p in pieces]
    rows = sum(sizes)
    feat = x.shape[0] if x_first else x.shape[1]
    tile = tile_of(width)
    count = len(pieces)

    def kernel(*refs):
        x_ref, parts, out_ref = refs[0], refs[1 : 1 + count], refs[-1]
        y = jnp.concatenate([p[...] for p in parts], axis=0)
        if x_first:
            out_ref[0] = dot(x_ref[...], y, 1, 0).astype(BF16)
        else:
            out_ref[0] = dot(y, x_ref[...], 0, 0).astype(BF16)

    if x_first:
        out_spec = pl.BlockSpec((1, feat, tile), lambda i: (j, 0, i))
    else:
        out_spec = pl.BlockSpec((1, tile, feat), lambda i: (j, i, 0))
    return pl.pallas_call(
        kernel,
        grid=(width // tile,),
        in_specs=[pl.BlockSpec(x.shape, lambda i: (0, 0))]
        + [pl.BlockSpec((n, tile), lambda i: (0, i)) for n in sizes]
        + unread(into)
        + unread(waits),
        out_specs=out_spec,
        out_shape=jax.ShapeDtypeStruct(shape, BF16),
        input_output_aliases={1 + count: 0} if into else {},
        name="outer",
        **(kernel_params(0, 0) if brief else kernel_params(2 * rows * feat * width, 2 * feat * width + 2 * rows * width)),
    )(x, *pieces, *into, *waits)


def spaced(*values):
    def kernel(*refs):
        refs[-1][...] = jnp.zeros_like(refs[-1])

    return pl.pallas_call(
        kernel,
        in_specs=unread(values),
        out_specs=pl.BlockSpec(memory_space=pltpu.VMEM),
        out_shape=jax.ShapeDtypeStruct((8, 128), F32),
        name="spaced",
        cost_estimate=pl.CostEstimate(flops=0, bytes_accessed=1 << 27, transcendentals=0),
    )(*values)


def gathered(values, waits):
    count = len(values)
    shape = (count,) + values[0].shape

    def kernel(*refs):
        for n in range(count):
            refs[-1][n] = refs[n][...]

    return pl.pallas_call(
        kernel,
        in_specs=[pl.BlockSpec(memory_space=pltpu.VMEM)] * count + unread(waits),
        out_specs=pl.BlockSpec(memory_space=pltpu.VMEM),
        out_shape=jax.ShapeDtypeStruct(shape, values[0].dtype),
        name="gathered",
        **kernel_params(0, 4 * count * values[0].size),
    )(*values, *waits)


def held(value, *waits):
    def kernel(*refs):
        refs[-1][...] = refs[0][...]

    return pl.pallas_call(
        kernel,
        in_specs=[pl.BlockSpec(memory_space=pltpu.VMEM)] + unread(waits),
        out_specs=pl.BlockSpec(memory_space=pltpu.VMEM),
        out_shape=jax.ShapeDtypeStruct(value.shape, value.dtype),
        name="held",
        **kernel_params(0, 4 * value.size),
    )(value, *waits)


def body(tokens, labels, grad_out, w_gate, w_up, w_down):
    local = w_gate.shape[0]
    groups = lax.axis_size("expert")
    cores = lax.axis_size("tensor")
    peers = lax.axis_size("dp")
    experts = local * groups
    rows = groups * MOST
    half, quarter = rows // 2, rows // 4
    share = MOST // cores
    part = MOST // 4
    paired = cores == 2
    me = lax.axis_index("dp")
    group = lax.axis_index("expert")
    core = lax.axis_index("tensor")

    def over_dp(value, bit):
        return lax.ppermute(value, "dp", [(i, i ^ bit) for i in range(peers)])

    def over_groups(value, shift):
        return lax.ppermute(value, "expert", [(i, (i + shift) % groups) for i in range(groups)])

    def other_core(value):
        return lax.ppermute(value, "tensor", [(0, 1), (1, 0)])

    first = [1 + j % 2 for j in range(local)]
    second = [2 - j % 2 for j in range(local)]

    domain = labels[:, 0]
    onehot = domain[:, None] == jnp.arange(experts, dtype=jnp.int32)[None, :]
    count = domain.shape[0]
    ahead = (jnp.arange(count)[:, None] > jnp.arange(count)[None, :]).astype(BF16)
    before = dot(ahead, onehot.astype(BF16), 1, 0)
    rank_in = jnp.sum(jnp.where(onehot, before, 0.0), axis=1).astype(jnp.int32)
    slot_of = rank_in * experts + domain

    def slots_held(of_core):
        place = jnp.arange(share, dtype=jnp.int32)[None, None, :]
        if not paired:
            place = place + of_core * share
        expert_in = jnp.arange(local, dtype=jnp.int32)[None, :, None]
        to_group = (group + jnp.arange(groups, dtype=jnp.int32)[:, None, None]) % groups
        bit_first = 1 + expert_in % 2
        bit_second = 2 - expert_in % 2
        position = place // part
        owner = (position // 2) * bit_first + (position % 2) * bit_second
        owner = owner ^ me
        if paired:
            owner = owner ^ (of_core * bit_first)
        rank = owner * part + place % part
        return (rank * experts + to_group * local + expert_in).reshape(-1)

    own_slots = slots_held(core)
    to_slots = (own_slots[:, None] == slot_of[None, :]).astype(BF16)

    def send_out(value):
        packed = dot(to_slots, value, 1, 0).astype(BF16).reshape(groups, local, share, -1)
        return [packed[0]] + [over_groups(packed[k], k) for k in range(1, groups)]

    def take_in(arrived):
        mine = jnp.stack(arrived)
        if paired:
            both = jnp.stack([mine, other_core(mine)])
        else:
            both = lax.all_gather(mine, "tensor", axis=0, tiled=False)
        inner = min(share, part)
        both = both.reshape(cores, groups, local, share // inner, inner, -1)
        both = both.transpose(2, 0, 3, 1, 4, 5).reshape(local, rows, -1)
        return [both[j] for j in range(local)]

    def send_half(source, weight, dim):
        return [dot(source[j][half:], weight[j], 1, dim).astype(BF16) for j in range(local)]

    def keep_half(source, weight, dim):
        return [dot(source[j][:half], weight[j], 1, dim) for j in range(local)]

    def step_one(sent):
        return [over_dp(sent[j], first[j]) for j in range(local)]

    def passed_on(kept, got):
        return [(kept[j][quarter:] + got[j][quarter:].astype(F32)).astype(BF16) for j in range(local)]

    def step_two(kept, got, passed):
        last = [over_dp(passed[j], second[j]) for j in range(local)]
        return [
            kept[j][:quarter] + got[j][:quarter].astype(F32) + last[j].astype(F32) for j in range(local)
        ]

    def along_second(value):
        return [over_dp(value[j], second[j]) for j in range(local)]

    def along_first(value):
        return [over_dp(value[j], first[j]) for j in range(local)]

    def rows_of(pieces, weight, dim, added=None, waits=()):
        return [
            back_to_rows(pieces[j], weight, j, dim, added[j] if added else (), waits) for j in range(local)
        ]

    def outer_all(source, pieces, shape, x_first, waits=(), brief=False):
        total = ()
        for j in range(local):
            total = (outer(source[j], pieces[j], shape, j, total, x_first, waits, brief),)
        return total[0]

    def share_blocks(value):
        width = value[0][0].shape[-1]
        if paired:
            summed = jnp.stack([low + other_core(high) for low, high in value])
        else:
            stacked = jnp.stack([jnp.concatenate(v, axis=0) for v in value])
            summed = lax.psum_scatter(stacked, "tensor", scatter_dimension=1, tiled=True)
        inner = min(share, part)
        summed = summed.astype(BF16).reshape(local, share // inner, groups, inner, width)
        blocks = summed.transpose(2, 0, 1, 3, 4).reshape(groups, local, share, width)
        return [blocks[k] for k in range(groups)]

    def return_home(blocks):
        return [blocks[0]] + [over_groups(blocks[k], -k) for k in range(1, groups)]

    def to_tokens(home):
        if paired:
            every = jnp.concatenate([home, other_core(home)], axis=0)
            held = jnp.concatenate([own_slots, slots_held(1 - core)])
        else:
            every = lax.all_gather(home, "tensor", axis=0, tiled=True)
            held = jnp.concatenate([slots_held(c) for c in range(cores)])
        from_slots = (slot_of[:, None] == held[None, :]).astype(BF16)
        return dot(from_slots, every, 1, 0).astype(BF16)

    inputs = take_in(send_out(tokens))
    gate_sent = send_half(inputs, w_gate, 0)
    gate_sent = list(lax.optimization_barrier(tuple(gate_sent)))
    gate_got = step_one(gate_sent)
    up_sent = send_half(inputs, w_up, 0)
    up_sent = list(lax.optimization_barrier(tuple(up_sent)))
    up_got = step_one(up_sent)
    grads_out = send_out(held(grad_out, *gate_sent))
    gate_kept = keep_half(inputs, w_gate, 0)
    gate_passed = passed_on(gate_kept, gate_got)
    gate_sum = step_two(gate_kept, gate_got, gate_passed)
    grad_rows = take_in(grads_out)
    up_kept = keep_half(inputs, w_up, 0)
    back_sent = send_half(grad_rows, w_down, 1)
    back_sent = list(lax.optimization_barrier(tuple(back_sent)))
    back_got = step_one(back_sent)
    back_kept = keep_half(grad_rows, w_down, 1)
    up_passed = passed_on(up_kept, up_got)
    up_sum = step_two(up_kept, up_got, up_passed)
    back_passed = passed_on(back_kept, back_got)

    hidden = []
    for j in range(local):
        hidden.append((gate_sum[j] * jax.nn.sigmoid(gate_sum[j]) * up_sum[j]).astype(BF16))
    h_second, h_first = along_second(hidden), along_first(hidden)
    back_sum = step_two(back_kept, back_got, back_passed)
    d_gate, d_up = [], []
    for j in range(local):
        g, u, b = gate_sum[j], up_sum[j], back_sum[j]
        s = jax.nn.sigmoid(g)
        d_gate.append((b * u * (s * (1.0 + g * (1.0 - s)))).astype(BF16))
        d_up.append((b * (g * s)).astype(BF16))

    h_both = along_first(h_second)
    late = [held(v, *h_both) for v in d_gate]
    g_second, g_first = along_second(late), along_first(late)
    hidden_pieces = list(zip(hidden, h_second, h_first, h_both))
    forward = rows_of(hidden_pieces, w_down, 0, None, g_second)
    g_both = along_first(g_second)
    late = d_up
    u_second, u_first = along_second(late), along_first(late)
    grad_down = outer_all(grad_rows, hidden_pieces, w_down.shape, False, [f[0] for f in forward] + u_second)
    gate_pieces = list(zip(d_gate, g_second, g_first, g_both))
    by_gate = rows_of(gate_pieces, w_gate, 1, None, ())
    inputs_t = [x.T for x in inputs]
    grad_gate = outer_all(inputs_t, gate_pieces, w_gate.shape, True, [grad_down])
    u_both = along_first(u_second)
    mixed_home = jnp.stack(return_home(share_blocks([(held(low, *g_both), high) for low, high in forward]))).reshape(
        groups * local * share, -1
    )
    mixed = to_tokens(mixed_home)
    up_pieces = list(zip(d_up, u_second, u_first, u_both))
    backward = rows_of(up_pieces, w_up, 1, by_gate, [grad_gate] + [mixed])
    grad_blocks = share_blocks(backward)
    grad_up = outer_all(inputs_t, up_pieces, w_up.shape, True, [spaced(*grad_blocks)], True)
    grad_home = gathered(return_home(grad_blocks), [grad_up])
    grad_tokens = to_tokens(grad_home.reshape(groups * local * share, -1))
    return mixed, grad_tokens, grad_gate, grad_up, grad_down


def solution(mesh):
    in_specs = (
        P("expert", "dp"),
        P("expert", None),
        P("expert", "dp"),
        P("expert", "dp", "tensor"),
        P("expert", "dp", "tensor"),
        P("expert", "tensor", "dp"),
    )
    out_specs = (
        P("expert", "dp"),
        P("expert", "dp"),
        P("expert", "dp", "tensor"),
        P("expert", "dp", "tensor"),
        P("expert", "tensor", "dp"),
    )
    return jax.shard_map(body, mesh=mesh, in_specs=in_specs, out_specs=out_specs, check_vma=False)
```
